32 devices in a mesh: grp: 2 (over x), sec: 16 (over z, y, core).
Axes of the slice: x: 2, y: 2, z: 4, core: 2. Of those that a mesh axis runs over, the one named last changes fastest.
Arguments:
- section_tile: bfloat16 [32, 512, 512], P(('grp', 'sec')), parts along dimension 0, may hold values from -8 to 8
- placement: int32 [64, 2], P('grp'), parts along dimension 0, may hold values from 0 to 384
- tissue_mask: int32 [32, 32], P(('grp', 'sec')), parts along dimension 0, may hold values 0 or 1
- level_use: int32 [3, 64], P(None, 'grp'), parts along dimension 1, may hold values 0 or 1
Outputs:
- flow_next: float32 [32, 2, 32], P(('grp', 'sec')), parts along dimension 0
- flow_skip: float32 [32, 2, 32], P(('grp', 'sec')), parts along dimension 0
- position: float32 [32, 2, 32], P(('grp', 'sec')), parts along dimension 0
The draws below stay inside these ranges and needn't reach their ends.
There are 2 independent parts, one for each index of `grp`. The reference program is written for one: setup_inputs(seed, part) draws one part's arguments, and reference() takes and returns one part's arrays. A program takes and returns all parts, laid end to end along the dimension named above; each array names one. Nothing has to cross between parts.
All inputs are finite; a program needn't handle non-finite values. No bound on the sum of `tissue_mask` on one device may be relied on, other than what follows from the above.
Results may differ from the reference program's by a relative error of at most 0.0044.
Values may be sent and summed in bfloat16 or wider, within the bound.
A program may use at most 128 MiB of HBM per device.

```python
import jax
import jax.numpy as jnp
from jax import lax

PATCH = 128
LEVELS = 3
P_SIZE = 32
TILE = 512
SEC = 16


def draw_section_tile(key, part):
    base_key = jax.random.fold_in(key, 11)
    shift_key = jax.random.fold_in(key, 12)
    noise_key = jax.random.fold_in(key, 13)
    offsets = jax.random.randint(shift_key, (SEC, 2), -4, 5)
    base = jax.random.normal(base_key, (TILE, TILE), jnp.float32)
    noise = 0.3 * jax.random.normal(noise_key, (SEC, TILE, TILE), jnp.float32)

    def one_section(offset, fresh):
        moved = jnp.roll(base, offset[0], axis=0)
        moved = jnp.roll(moved, offset[1], axis=1)
        return moved + fresh
    tiles = jax.vmap(one_section)(offsets, noise)
    return jnp.clip(tiles, -8.0, 8.0).astype(jnp.bfloat16)


def set_ends(values, key, least, top_value):
    place = [jax.random.randint(jax.random.fold_in(key, axis), (), 0, length) for axis, length in enumerate(values.shape)]
    widest = values.shape.index(max(values.shape))
    beside = place[:widest] + [(place[widest] + 1) % values.shape[widest]] + place[widest + 1:]
    return values.at[tuple(place)].set(least).at[tuple(beside)].set(top_value)


def setup_inputs(seed: int = 0, part: int = 0) -> dict:
    key_list = jax.random.split(jax.random.key(seed), 5)
    part_splits = jax.random.split(jax.random.fold_in(key_list[4], part), 5)
    section_tile = draw_section_tile(jax.random.fold_in(jax.random.fold_in(key_list[4], part), 71), part)
    placement = set_ends(jax.random.randint(part_splits[1], (P_SIZE, 2), 0, TILE - PATCH + 1), jax.random.fold_in(part_splits[1], 1), 0, TILE - PATCH).astype(jnp.int32)
    tissue_mask = set_ends((jax.random.randint(part_splits[2], (SEC, P_SIZE), 0, 4) < 3).astype(jnp.int32), jax.random.fold_in(part_splits[2], 1), 0, 1)
    level_use = set_ends((jax.random.randint(part_splits[3], (LEVELS, P_SIZE), 0, 3) < 2).astype(jnp.int32), jax.random.fold_in(part_splits[3], 1), 0, 1)
    return {"section_tile": section_tile, "placement": placement, "tissue_mask": tissue_mask, "level_use": level_use}


def dft_tables():
    index = jnp.arange(PATCH, dtype=jnp.int32)
    product = (index[:, None] * index[None, :]) % PATCH
    angles = product.astype(jnp.float32) * (2.0 * jnp.pi / PATCH)
    return jnp.cos(angles).astype(jnp.bfloat16), (-jnp.sin(angles)).astype(jnp.bfloat16)


def band_vector(level_number):
    index = jnp.arange(PATCH, dtype=jnp.int32)
    signed_freq = jnp.minimum(index, PATCH - index)
    return (signed_freq < PATCH // 2 ** (level_number + 1)).astype(jnp.float32)


def offset_vector():
    index = jnp.arange(PATCH, dtype=jnp.int32)
    return jnp.where(index < PATCH // 2, index, index - PATCH).astype(jnp.float32)


def extract(plane, placement):
    def one_patch(corner):
        return lax.dynamic_slice(plane, (corner[0], corner[1]), (PATCH, PATCH))
    return jax.vmap(one_patch)(placement.astype(jnp.int32))


def blend_terms(form, left, right):
    return jnp.einsum(form, left.astype(jnp.float32), right.astype(jnp.float32))


def spectrum(patches, cosine_lookup, sine_lookup):
    real_rows = blend_terms("kn,pnm->pkm", cosine_lookup, patches).astype(jnp.bfloat16)
    imag_rows = blend_terms("kn,pnm->pkm", sine_lookup, patches).astype(jnp.bfloat16)
    spec_real = (blend_terms("pkm,ml->pkl", real_rows, cosine_lookup) - blend_terms("pkm,ml->pkl", imag_rows, sine_lookup)) / PATCH
    spec_imag = (blend_terms("pkm,ml->pkl", real_rows, sine_lookup) + blend_terms("pkm,ml->pkl", imag_rows, cosine_lookup)) / PATCH
    return spec_real.astype(jnp.bfloat16), spec_imag.astype(jnp.bfloat16)


def centroid(correl, offsets):
    weights = correl * correl
    total = jnp.sum(weights, axis=(1, 2)) + 1e-6
    along_rows = jnp.sum(weights * offsets[None, :, None], axis=(1, 2)) / total
    along_cols = jnp.sum(weights * offsets[None, None, :], axis=(1, 2)) / total
    return jnp.stack([along_rows, along_cols])


def pair_flow(own_real, own_imag, other_real, other_imag, cosine_lookup, sine_lookup, usage, valid):
    first_real = own_real.astype(jnp.float32)
    first_imag = own_imag.astype(jnp.float32)
    second_real = other_real.astype(jnp.float32)
    second_imag = other_imag.astype(jnp.float32)
    cross_power_real = (first_real * second_real + first_imag * second_imag).astype(jnp.bfloat16)
    cross_power_imaginary = (first_imag * second_real - first_real * second_imag).astype(jnp.bfloat16)
    offsets = offset_vector()
    estimate = jnp.zeros((2, usage.shape[1]), jnp.float32)
    for level_number in range(LEVELS):
        band_row = band_vector(level_number)
        window = band_row[:, None] * band_row[None, :]
        tissue_real = cross_power_real.astype(jnp.float32) * window
        tissue_imaginary = cross_power_imaginary.astype(jnp.float32) * window
        partial_real = (blend_terms("dt,hts->hds", cosine_lookup, tissue_real) + blend_terms("dt,hts->hds", sine_lookup, tissue_imaginary)).astype(jnp.bfloat16)
        partial_imaginary = (blend_terms("dt,hts->hds", cosine_lookup, tissue_imaginary) - blend_terms("dt,hts->hds", sine_lookup, tissue_real)).astype(jnp.bfloat16)
        correl = (blend_terms("pkq,ql->pkl", partial_real, cosine_lookup) + blend_terms("pkq,ql->pkl", partial_imaginary, sine_lookup)) / PATCH
        estimate = estimate + usage[level_number][None, :] * centroid(correl, offsets)
    count = jnp.maximum(jnp.sum(usage, axis=0), 1.0)
    return valid[None, :] * estimate / count[None, :]


def shifted(values, step):
    padding = jnp.zeros_like(values[:step])
    return jnp.concatenate([values[step:], padding], axis=0)


def reference(section_tile, placement, tissue_mask, level_use):
    cosine_lookup, sine_lookup = dft_tables()

    def section_spectra(plane):
        return spectrum(extract(plane, placement), cosine_lookup, sine_lookup)

    spec_real, spec_imag = lax.map(section_spectra, section_tile)
    flags = tissue_mask.astype(jnp.float32)
    usage = level_use.astype(jnp.float32)

    def flows_at(step):
        def one_section(items):
            own_real, own_imag, other_real, other_imag, own_flag, other_flag = items
            return pair_flow(own_real, own_imag, other_real, other_imag, cosine_lookup, sine_lookup, usage, own_flag * other_flag)
        return lax.map(one_section, (spec_real, spec_imag, shifted(spec_real, step), shifted(spec_imag, step), flags, shifted(flags, step)))

    flow_next = flows_at(1)
    flow_skip = flows_at(2)
    position = jnp.cumsum(flow_next, axis=0)
    return flow_next, flow_skip, position
```

```python
import functools

import jax
import jax.numpy as jnp
import ml_dtypes
import numpy as np
from jax import lax
from jax.experimental import pallas as pl
from jax.experimental.pallas import tpu as pltpu
from jax.sharding import PartitionSpec as P

PATCH = 128
HALF = PATCH // 2
LEVELS = 3
MESH = pl.DeviceIdType.MESH


def tables():
    index = np.arange(PATCH)
    product = (index[:, None] * index[None, :]) % PATCH
    angles = product.astype(np.float32) * np.float32(2.0 * np.pi / PATCH)
    cos = np.cos(angles).astype(ml_dtypes.bfloat16).astype(np.float32)
    sin = (-np.sin(angles)).astype(ml_dtypes.bfloat16).astype(np.float32)

    rows = np.concatenate([cos[:HALF], sin[:HALF]], axis=0)

    def two(block):
        zero = np.zeros_like(block)
        return np.block([[block, zero], [zero, block]])

    c, s = cos[:, :HALF] / PATCH, sin[:, :HALF] / PATCH
    cols = np.stack(
        [np.concatenate([two(c), two(s)], 1), np.concatenate([two(-s), two(c)], 1)]
    )

    freq = np.concatenate([np.arange(HALF), (-np.arange(HALF)) % PATCH])
    used = (np.arange(PATCH) != HALF).astype(np.float32)
    first, second = [], []
    for level in range(LEVELS):
        band = (np.arange(HALF) < PATCH // 2 ** (level + 1)).astype(np.float32)
        keep = np.concatenate([band, band]) * used
        c, s = cos[:, freq] * keep, sin[:, freq] * keep
        first.append(np.block([[c, s], [-s, c]]))
        weight = (np.where(np.arange(HALF) == 0, 1.0, 2.0) / PATCH * band)[:, None]
        second.append(
            np.concatenate([two(cos[:HALF] * weight), two(sin[:HALF] * weight)], 0)
        )
    first = np.concatenate(first, 0)
    second = np.stack(second)
    return tuple(t.astype(ml_dtypes.bfloat16) for t in (rows, cols, first, second))


def dot(a, b):
    return jnp.dot(a, b, preferred_element_type=jnp.float32)


def centre(position):
    return 8 * position if 8 * position < HALF else 8 * position - PATCH


def kernel(
    n, tile_ref, place_ref, mask_ref, use_ref, rows_ref, cols_ref, first_ref, second_ref,
    next_ref, skip_ref, pos_ref,
    wide, got, got_mask, own, totals, moments, mine, earlier,
    tile_send, tile_recv, mask_send, mask_recv, flow_send, flow_recv,
):
    me = lax.axis_index("sec")
    grp = lax.axis_index("grp")
    patches = use_ref.shape[1]
    pairs = patches // 2
    side = tile_ref.shape[1]

    barrier = pltpu.get_barrier_semaphore()

    def greet(step, _):
        other = lax.rem(me + step, n)
        pl.semaphore_signal(barrier, inc=1, device_id=(grp, other), device_id_type=MESH)
        return 0

    lax.fori_loop(1, n, greet, 0)
    pl.semaphore_wait(barrier, n - 1)

    def tile_copy(gap):
        return pltpu.make_async_remote_copy(
            src_ref=tile_ref.at[0], dst_ref=got.at[gap - 1],
            send_sem=tile_send.at[gap - 1], recv_sem=tile_recv.at[gap - 1],
            device_id=(grp, me - gap), device_id_type=MESH,
        )

    def mask_copy(gap):
        return pltpu.make_async_remote_copy(
            src_ref=mask_ref, dst_ref=got_mask.at[gap - 1],
            send_sem=mask_send.at[gap - 1], recv_sem=mask_recv.at[gap - 1],
            device_id=(grp, me - gap), device_id_type=MESH,
        )

    for gap in (1, 2):
        @pl.when(me >= gap)
        def _(gap=gap):
            tile_copy(gap).start()
            mask_copy(gap).start()

    lane = lax.broadcasted_iota(jnp.int32, (PATCH, PATCH), 1)

    def patch(p):
        row, col = place_ref[p, 0], place_ref[p, 1]
        block = lax.div(col, PATCH)
        within = lax.rem(col, PATCH)
        a = wide[block, pl.ds(row, PATCH), :]
        b = wide[jnp.minimum(block + 1, side // PATCH - 1), pl.ds(row, PATCH), :]
        mixed = jnp.where(lane >= within, a, b)
        shift = lax.rem(PATCH - within, PATCH)
        return pltpu.roll(mixed, shift, 1).astype(jnp.bfloat16)

    def spectra(q):
        halves = []
        for pair in (q, q + 1):
            both = jnp.concatenate([patch(pair), patch(pair + pairs)], axis=1)
            halves.append(dot(rows_ref[...], both).astype(jnp.bfloat16))
        u = dot(jnp.concatenate([h[:HALF] for h in halves], 0), cols_ref[0])
        v = dot(jnp.concatenate([h[HALF:] for h in halves], 0), cols_ref[1])
        plus, minus = (u + v).astype(jnp.bfloat16), (u - v).astype(jnp.bfloat16)
        return [
            jnp.concatenate([plus[HALF * i:HALF * (i + 1)], minus[HALF * i:HALF * (i + 1)]], 0)
            for i in (0, 1)
        ]

    def own_quad(i, _):
        for j, value in enumerate(spectra(2 * i)):
            own[2 * i + j] = value
        return 0

    sub = lax.broadcasted_iota(jnp.int32, (8, 2 * PATCH), 0).astype(jnp.float32)

    def pair_quad(i, _):
        q = 2 * i
        real, imag = [], []
        for j, other in enumerate(spectra(q)):
            mine_ = own[q + j].astype(jnp.float32)
            other = other.astype(jnp.float32)
            ar, ai = mine_[:, :PATCH], mine_[:, PATCH:]
            br, bi = other[:, :PATCH], other[:, PATCH:]
            real.append((ar * br + ai * bi).astype(jnp.bfloat16))
            imag.append((ai * br - ar * bi).astype(jnp.bfloat16))
        cross = jnp.concatenate(
            [jnp.concatenate(real, 1), jnp.concatenate(imag, 1)], 0
        )
        for level in range(LEVELS):
            half = dot(
                first_ref[pl.ds(2 * PATCH * level, 2 * PATCH)], cross
            ).astype(jnp.bfloat16)
            for j in (0, 1):
                lanes = slice(PATCH * j, PATCH * (j + 1))
                both = jnp.concatenate([half[:PATCH, lanes], half[PATCH:, lanes]], 1)
                correl = dot(both, second_ref[level])
                weights = correl * correl
                total = jnp.zeros((8, 2 * PATCH), jnp.float32)
                moment = jnp.zeros((8, 2 * PATCH), jnp.float32)
                for g in range(PATCH // 8):
                    w = weights[8 * g:8 * (g + 1)]
                    total = total + w
                    if centre(g):
                        moment = moment + w * float(centre(g))
                moment = moment + sub * total
                total = jnp.sum(total, 0, keepdims=True)
                moment = jnp.sum(moment, 0, keepdims=True)
                for h in (0, 1):
                    lanes_ = slice(PATCH * h, PATCH * (h + 1))
                    totals[level, pl.ds(q + j + h * pairs, 1), :] = total[:, lanes_]
                    moments[level, pl.ds(q + j + h * pairs, 1), :] = moment[:, lanes_]
        return 0

    position = lax.broadcasted_iota(jnp.int32, (8, PATCH), 1)
    offset = jnp.where(position < HALF, position, position - PATCH).astype(jnp.float32)
    which = lax.broadcasted_iota(jnp.int32, (8, PATCH), 0)
    gather = jnp.where(which == 0, 1.0, jnp.where(which == 1, offset, 0.0))

    def over_lanes(values):
        return lax.dot_general(
            gather, values, (((1,), (1,)), ((), ())),
            precision=lax.Precision.HIGHEST, preferred_element_type=jnp.float32,
        )

    def flow(gap):
        usage = use_ref[...].astype(jnp.float32)
        along_rows = jnp.zeros((1, patches), jnp.float32)
        along_cols = jnp.zeros((1, patches), jnp.float32)
        for level in range(LEVELS):
            whole = over_lanes(totals[level])
            slope = over_lanes(moments[level])
            use = usage[level:level + 1]
            norm = whole[0:1] + 1e-06
            along_rows = along_rows + use * (slope[0:1] / norm)
            along_cols = along_cols + use * (whole[1:2] / norm)
        count = jnp.maximum(jnp.sum(usage, axis=0, keepdims=True), 1.0)
        valid = mask_ref[...].astype(jnp.float32) * got_mask[gap - 1].astype(jnp.float32)
        both = jnp.concatenate([along_rows, along_cols], 0)
        return valid * both / count

    def widen(plane):
        for block in range(side // PATCH):
            lanes = pl.ds(PATCH * block, PATCH)
            wide[block] = plane[:, lanes].astype(jnp.float32)

    widen(tile_ref.at[0])
    lax.fori_loop(0, pairs // 2, own_quad, 0)

    def flow_copy(other):
        return pltpu.make_async_remote_copy(
            src_ref=mine, dst_ref=earlier.at[me],
            send_sem=flow_send.at[other], recv_sem=flow_recv.at[me],
            device_id=(grp, other), device_id_type=MESH,
        )

    for gap, out in ((1, next_ref), (2, skip_ref)):
        @pl.when(me + gap < n)
        def _(gap=gap, out=out):
            tile_copy(gap).wait_recv()
            mask_copy(gap).wait_recv()
            widen(got.at[gap - 1])
            lax.fori_loop(0, pairs // 2, pair_quad, 0)
            out[0] = flow(gap)

        @pl.when(me + gap >= n)
        def _(out=out):
            out[...] = jnp.zeros_like(out)

        if gap == 1:
            mine[...] = out[0]

            def send(other, _):
                flow_copy(other).start()
                return 0

            lax.fori_loop(me + 1, n, send, 0)

    def arrived(t, state):
        pltpu.make_async_remote_copy(
            src_ref=mine, dst_ref=earlier.at[t],
            send_sem=flow_send.at[t], recv_sem=flow_recv.at[t],
            device_id=(grp, me), device_id_type=MESH,
        ).wait_recv()
        return state + earlier[t]

    before = lax.fori_loop(0, me, arrived, jnp.zeros(mine.shape, jnp.float32))
    pos_ref[0] = before + mine[...]

    def sent(other, _):
        flow_copy(other).wait_send()
        return 0

    lax.fori_loop(me + 1, n, sent, 0)
    for gap in (1, 2):
        @pl.when(me >= gap)
        def _(gap=gap):
            tile_copy(gap).wait_send()
            mask_copy(gap).wait_send()


def on_device(n, section_tile, placement, tissue_mask, level_use):
    side = section_tile.shape[1]
    patches = placement.shape[0]
    out = jax.ShapeDtypeStruct((1, 2, patches), jnp.float32)
    vmem = pl.BlockSpec(memory_space=pltpu.VMEM)
    smem = pl.BlockSpec(memory_space=pltpu.SMEM)
    dma = pltpu.SemaphoreType.DMA
    return pl.pallas_call(
        functools.partial(kernel, n),
        out_shape=(out, out, out),
        in_specs=[vmem, smem] + [vmem] * 6,
        out_specs=(vmem, vmem, vmem),
        scratch_shapes=[
            pltpu.VMEM((side // PATCH, side, PATCH), jnp.float32),
            pltpu.VMEM((2, side, side), jnp.bfloat16),
            pltpu.VMEM((2, 1, patches), jnp.int32),
            pltpu.VMEM((patches // 2, PATCH, 2 * PATCH), jnp.bfloat16),
            pltpu.VMEM((LEVELS, patches, PATCH), jnp.float32),
            pltpu.VMEM((LEVELS, patches, PATCH), jnp.float32),
            pltpu.VMEM((2, patches), jnp.float32),
            pltpu.VMEM((n, 2, patches), jnp.float32),
            dma((2,)), dma((2,)), dma((2,)), dma((2,)), dma((n,)), dma((n,)),
        ],
        compiler_params=pltpu.CompilerParams(
            collective_id=0, has_side_effects=True, vmem_limit_bytes=40 * 2**20
        ),
    )(section_tile, placement, tissue_mask, level_use, *[jnp.asarray(t) for t in tables()])


def solution(mesh):
    in_specs = (
        P(("grp", "sec"), None, None),
        P("grp", None),
        P(("grp", "sec"), None),
        P(None, "grp"),
    )
    out_specs = (P(("grp", "sec"), None, None),) * 3
    return jax.shard_map(
        functools.partial(on_device, mesh.shape["sec"]),
        mesh=mesh, in_specs=in_specs, out_specs=out_specs, check_vma=False,
    )
```

```python
import functools

import jax
import jax.numpy as jnp
import ml_dtypes
import numpy as np
from jax import lax
from jax.experimental import pallas as pl
from jax.experimental.pallas import tpu as pltpu
from jax.sharding import PartitionSpec as P

PATCH = 128
HALF = PATCH // 2
LEVELS = 3
GROUP = 4
MESH = pl.DeviceIdType.MESH


def tables():
    index = np.arange(PATCH)
    product = (index[:, None] * index[None, :]) % PATCH
    angles = product.astype(np.float32) * np.float32(2.0 * np.pi / PATCH)
    cos = np.cos(angles).astype(ml_dtypes.bfloat16).astype(np.float32)
    sin = (-np.sin(angles)).astype(ml_dtypes.bfloat16).astype(np.float32)

    rows = np.concatenate([cos[:HALF], sin[:HALF]], axis=0)

    def two(block):
        zero = np.zeros_like(block)
        return np.block([[block, zero], [zero, block]])

    c, s = cos[:, :HALF] / PATCH, sin[:, :HALF] / PATCH
    cols = np.stack(
        [np.concatenate([two(c), two(s)], 1), np.concatenate([two(-s), two(c)], 1)]
    )

    freq = np.concatenate([np.arange(HALF), (-np.arange(HALF)) % PATCH])
    used = (np.arange(PATCH) != HALF).astype(np.float32)
    first, second = [], []
    for level in range(LEVELS):
        band = (np.arange(HALF) < PATCH // 2 ** (level + 1)).astype(np.float32)
        keep = np.concatenate([band, band]) * used
        c, s = cos[:, freq] * keep, sin[:, freq] * keep
        first.append(np.block([[c, s], [-s, c]]))
        weight = (np.where(np.arange(HALF) == 0, 1.0, 2.0) / PATCH * band)[:, None]
        second.append(
            np.concatenate([two(cos[:HALF] * weight), two(sin[:HALF] * weight)], 0)
        )
    first = np.concatenate(first, 0)
    second = np.stack(second)
    return tuple(t.astype(ml_dtypes.bfloat16) for t in (rows, cols, first, second))


def dot(a, b):
    return jnp.dot(a, b, preferred_element_type=jnp.float32)


def centre(position):
    return 8 * position if 8 * position < HALF else 8 * position - PATCH


def kernel(
    n, tile_hbm, place_hbm, mask_ref, use_ref, rows_hbm, cols_hbm, first_hbm, second_hbm,
    out_ref,
    tile_ref, place_ref, rows_ref, cols_ref, first_ref, second_ref, load_sem,
    wide, got, got_mask, own, totals, moments, mine, earlier,
    tile_send, tile_recv, mask_send, mask_recv, flow_send, flow_recv, go,
):
    me = lax.axis_index("sec")
    grp = lax.axis_index("grp")
    patches = use_ref.shape[1]
    pairs = patches // 2
    group = GROUP if pairs % GROUP == 0 else 2
    side = tile_ref.shape[1]

    loads = [
        pltpu.make_async_copy(src, dst, load_sem.at[i])
        for i, (src, dst) in enumerate((
            (tile_hbm, tile_ref), (place_hbm, place_ref), (rows_hbm, rows_ref),
            (cols_hbm, cols_ref), (first_hbm, first_ref), (second_hbm, second_ref),
        ))
    ]
    for load in loads:
        load.start()

    barrier = pltpu.get_barrier_semaphore()

    def greet(step, _):
        other = lax.rem(me + step, n)
        pl.semaphore_signal(barrier, inc=1, device_id=(grp, other), device_id_type=MESH)
        return 0

    lax.fori_loop(1, n, greet, 0)
    loads[0].wait()
    pl.semaphore_wait(barrier, n - 1)

    def tile_copy(gap):
        return pltpu.make_async_remote_copy(
            src_ref=tile_ref.at[0], dst_ref=got.at[gap - 1],
            send_sem=tile_send.at[gap - 1], recv_sem=tile_recv.at[gap - 1],
            device_id=(grp, me - gap), device_id_type=MESH,
        )

    def mask_copy(gap):
        return pltpu.make_async_remote_copy(
            src_ref=mask_ref, dst_ref=got_mask.at[gap - 1],
            send_sem=mask_send.at[gap - 1], recv_sem=mask_recv.at[gap - 1],
            device_id=(grp, me - gap), device_id_type=MESH,
        )

    odd = lax.rem(me, 2) == 1
    relays = jnp.logical_and(odd, me + 1 < n)
    skips = jnp.logical_and(odd, me >= 2)

    def relay_copy():
        return pltpu.make_async_remote_copy(
            src_ref=got.at[0], dst_ref=got.at[1],
            send_sem=tile_send.at[2], recv_sem=tile_recv.at[1],
            device_id=(grp, me - 1), device_id_type=MESH,
        )

    for gap in (1, 2):
        @pl.when(me >= gap)
        def _(gap=gap):
            if gap == 1:
                tile_copy(gap).start()
            mask_copy(gap).start()

    lane = lax.broadcasted_iota(jnp.int32, (PATCH, PATCH), 1)

    def patch(p):
        row, col = place_ref[0, p], place_ref[1, p]
        block = lax.div(col, PATCH)
        within = lax.rem(col, PATCH)
        a = wide[block, pl.ds(row, PATCH), :]
        b = wide[jnp.minimum(block + 1, side // PATCH - 1), pl.ds(row, PATCH), :]
        mixed = jnp.where(lane >= within, a, b)
        shift = lax.rem(PATCH - within, PATCH)
        return pltpu.roll(mixed, shift, 1).astype(jnp.bfloat16)

    def spectra(q):
        halves = []
        for pair in range(group):
            both = jnp.concatenate([patch(q + pair), patch(q + pair + pairs)], axis=1)
            halves.append(dot(rows_ref[...], both).astype(jnp.bfloat16))
        u = dot(jnp.concatenate([h[:HALF] for h in halves], 0), cols_ref[0])
        v = dot(jnp.concatenate([h[HALF:] for h in halves], 0), cols_ref[1])
        plus, minus = (u + v).astype(jnp.bfloat16), (u - v).astype(jnp.bfloat16)
        return [
            jnp.concatenate([plus[HALF * i:HALF * (i + 1)], minus[HALF * i:HALF * (i + 1)]], 0)
            for i in range(group)
        ]

    def own_quad(i, _):
        for j, value in enumerate(spectra(group * i)):
            own[group * i + j] = value
        return 0

    sub = lax.broadcasted_iota(jnp.int32, (8, 2 * PATCH), 0).astype(jnp.float32)

    def pair_quad(i, _):
        q = group * i
        real, imag = [], []
        for j, other in enumerate(spectra(q)):
            mine_ = own[q + j].astype(jnp.float32)
            other = other.astype(jnp.float32)
            ar, ai = mine_[:, :PATCH], mine_[:, PATCH:]
            br, bi = other[:, :PATCH], other[:, PATCH:]
            real.append((ar * br + ai * bi).astype(jnp.bfloat16))
            imag.append((ai * br - ar * bi).astype(jnp.bfloat16))
        halves = []
        for j in range(0, group, 2):
            cross = jnp.concatenate(
                [jnp.concatenate(real[j:j + 2], 1), jnp.concatenate(imag[j:j + 2], 1)], 0
            )
            halves.append(dot(first_ref[...], cross).astype(jnp.bfloat16))
        for level in range(LEVELS):
            top = 2 * PATCH * level
            both = jnp.concatenate([
                jnp.concatenate([half[top:top + PATCH, lanes], half[top + PATCH:top + 2 * PATCH, lanes]], 1)
                for half in halves for lanes in (slice(0, PATCH), slice(PATCH, 2 * PATCH))
            ], 0)
            correl = dot(both, second_ref[level])
            for j in range(group):
                weights = correl[PATCH * j:PATCH * (j + 1)]
                weights = weights * weights
                total = jnp.zeros((8, 2 * PATCH), jnp.float32)
                moment = jnp.zeros((8, 2 * PATCH), jnp.float32)
                for g in range(PATCH // 8):
                    w = weights[8 * g:8 * (g + 1)]
                    total = total + w
                    if centre(g):
                        moment = moment + w * float(centre(g))
                moment = moment + sub * total
                total = jnp.sum(total, 0, keepdims=True)
                moment = jnp.sum(moment, 0, keepdims=True)
                for h in (0, 1):
                    lanes = slice(PATCH * h, PATCH * (h + 1))
                    totals[level, pl.ds(q + j + h * pairs, 1), :] = total[:, lanes]
                    moments[level, pl.ds(q + j + h * pairs, 1), :] = moment[:, lanes]
        return 0

    position = lax.broadcasted_iota(jnp.int32, (8, PATCH), 1)
    offset = jnp.where(position < HALF, position, position - PATCH).astype(jnp.float32)
    which = lax.broadcasted_iota(jnp.int32, (8, PATCH), 0)
    gather = jnp.where(which == 0, 1.0, jnp.where(which == 1, offset, 0.0))

    def over_lanes(values):
        return lax.dot_general(
            gather, values, (((1,), (1,)), ((), ())),
            precision=lax.Precision.HIGHEST, preferred_element_type=jnp.float32,
        )

    def flow(gap):
        usage = use_ref[...].astype(jnp.float32)
        along_rows = jnp.zeros((1, patches), jnp.float32)
        along_cols = jnp.zeros((1, patches), jnp.float32)
        for level in range(LEVELS):
            whole = over_lanes(totals[level])
            slope = over_lanes(moments[level])
            use = usage[level:level + 1]
            norm = whole[0:1] + 1e-06
            along_rows = along_rows + use * (slope[0:1] / norm)
            along_cols = along_cols + use * (whole[1:2] / norm)
        count = jnp.maximum(jnp.sum(usage, axis=0, keepdims=True), 1.0)
        valid = mask_ref[...].astype(jnp.float32) * got_mask[gap - 1].astype(jnp.float32)
        both = jnp.concatenate([along_rows, along_cols], 0)
        return valid * both / count

    def widen(plane):
        for block in range(side // PATCH):
            lanes = pl.ds(PATCH * block, PATCH)
            wide[block] = plane[:, lanes].astype(jnp.float32)

    widen(tile_ref.at[0])
    for load in loads[1:]:
        load.wait()
    lax.fori_loop(0, pairs // group, own_quad, 0, unroll=2)

    last_pair = jnp.logical_and(me == n - 2, jnp.logical_and(jnp.logical_not(odd), me >= 1))

    @pl.when(last_pair)
    def _():
        tile_copy(1).wait_send()
        pl.semaphore_signal(go, inc=1, device_id=(grp, me + 1), device_id_type=MESH)

    def flow_copy(other):
        return pltpu.make_async_remote_copy(
            src_ref=mine, dst_ref=earlier.at[me],
            send_sem=flow_send.at[other], recv_sem=flow_recv.at[me],
            device_id=(grp, other), device_id_type=MESH,
        )

    for gap, out in ((1, out_ref.at[0]), (2, out_ref.at[1])):
        @pl.when(me + gap < n)
        def _(gap=gap, out=out):
            tile_copy(gap).wait_recv()
            if gap == 1:
                pl.when(relays)(lambda: relay_copy().start())
                pl.when(skips)(lambda: tile_copy(2).start())
            mask_copy(gap).wait_recv()
            widen(got.at[gap - 1])
            lax.fori_loop(0, pairs // group, pair_quad, 0, unroll=2)
            out[0] = flow(gap)

        @pl.when(me + gap >= n)
        def _(gap=gap, out=out):
            if gap == 1:
                @pl.when(skips)
                def _():
                    pl.semaphore_wait(go, 1)
                    tile_copy(2).start()
            out[...] = jnp.zeros_like(out)

        if gap == 1:
            mine[...] = out[0]

            def send(other, _):
                flow_copy(other).start()
                return 0

            lax.fori_loop(me + 1, n, send, 0)

    def arrived(t, state):
        pltpu.make_async_remote_copy(
            src_ref=mine, dst_ref=earlier.at[t],
            send_sem=flow_send.at[t], recv_sem=flow_recv.at[t],
            device_id=(grp, me), device_id_type=MESH,
        ).wait_recv()
        return state + earlier[t]

    before = lax.fori_loop(0, me, arrived, jnp.zeros(mine.shape, jnp.float32))
    out_ref[2, 0] = before + mine[...]

    def sent(other, _):
        flow_copy(other).wait_send()
        return 0

    lax.fori_loop(me + 1, n, sent, 0)
    for gap in (1, 2):
        @pl.when(me >= gap)
        def _(gap=gap):
            if gap == 1:
                pl.when(jnp.logical_not(last_pair))(lambda: tile_copy(1).wait_send())
            mask_copy(gap).wait_send()
    pl.when(relays)(lambda: relay_copy().wait_send())
    pl.when(skips)(lambda: tile_copy(2).wait_send())


def on_device(n, section_tile, placement, tissue_mask, level_use):
    side = section_tile.shape[1]
    patches = placement.shape[0]
    out = jax.ShapeDtypeStruct((3, 1, 2, patches), jnp.float32)
    vmem = pl.BlockSpec(memory_space=pltpu.VMEM)
    dma = pltpu.SemaphoreType.DMA
    consts = [jnp.asarray(t) for t in tables()]
    anywhere = pl.BlockSpec(memory_space=pl.ANY)
    flows = pl.pallas_call(
        functools.partial(kernel, n),
        out_shape=out,
        in_specs=[anywhere] * 2 + [vmem] * 2 + [anywhere] * 4,
        out_specs=vmem,
        scratch_shapes=[
            pltpu.VMEM(section_tile.shape, section_tile.dtype),
            pltpu.SMEM((2, patches), placement.dtype),
            *[pltpu.VMEM(t.shape, t.dtype) for t in consts],
            dma((6,)),
            pltpu.VMEM((side // PATCH, side, PATCH), jnp.float32),
            pltpu.VMEM((2, side, side), jnp.bfloat16),
            pltpu.VMEM((2, 1, patches), jnp.int32),
            pltpu.VMEM((patches // 2, PATCH, 2 * PATCH), jnp.bfloat16),
            pltpu.VMEM((LEVELS, patches, PATCH), jnp.float32),
            pltpu.VMEM((LEVELS, patches, PATCH), jnp.float32),
            pltpu.VMEM((2, patches), jnp.float32),
            pltpu.VMEM((n, 2, patches), jnp.float32),
            dma((3,)), dma((2,)), dma((2,)), dma((2,)), dma((n,)), dma((n,)), pltpu.SemaphoreType.REGULAR,
        ],
        compiler_params=pltpu.CompilerParams(
            collective_id=0, has_side_effects=True, vmem_limit_bytes=56 * 2**20
        ),
    )(section_tile, placement.T, tissue_mask, level_use, *consts)
    return flows[0], flows[1], flows[2]


def solution(mesh):
    in_specs = (
        P(("grp", "sec"), None, None),
        P("grp", None),
        P(("grp", "sec"), None),
        P(None, "grp"),
    )
    out_specs = (P(("grp", "sec"), None, None),) * 3
    return jax.shard_map(
        functools.partial(on_device, mesh.shape["sec"]),
        mesh=mesh, in_specs=in_specs, out_specs=out_specs, check_vma=False,
    )
```

```python
import functools

import jax
import jax.numpy as jnp
import ml_dtypes
import numpy as np
from jax import lax
from jax.experimental import pallas as pl
from jax.experimental.pallas import tpu as pltpu
from jax.sharding import PartitionSpec as P

PATCH = 128
HALF = PATCH // 2
LEVELS = 3
GROUP = 4
MESH = pl.DeviceIdType.MESH


def tables():
    index = np.arange(PATCH)
    product = (index[:, None] * index[None, :]) % PATCH
    angles = product.astype(np.float32) * np.float32(2.0 * np.pi / PATCH)
    cos = np.cos(angles).astype(ml_dtypes.bfloat16).astype(np.float32)
    sin = (-np.sin(angles)).astype(ml_dtypes.bfloat16).astype(np.float32)

    rows = np.concatenate([cos[:HALF], sin[:HALF]], axis=0)

    def two(block):
        zero = np.zeros_like(block)
        return np.block([[block, zero], [zero, block]])

    c, s = cos[:, :HALF] / PATCH, sin[:, :HALF] / PATCH
    cols = np.stack(
        [np.concatenate([two(c), two(s)], 1), np.concatenate([two(-s), two(c)], 1)]
    )

    freq = np.concatenate([np.arange(HALF), (-np.arange(HALF)) % PATCH])
    used = (np.arange(PATCH) != HALF).astype(np.float32)
    first, second = [], []
    for level in range(LEVELS):
        band = (np.arange(HALF) < PATCH // 2 ** (level + 1)).astype(np.float32)
        keep = np.concatenate([band, band]) * used
        c, s = cos[:, freq] * keep, sin[:, freq] * keep
        first.append(np.block([[c, s], [-s, c]]))
        weight = (np.where(np.arange(HALF) == 0, 1.0, 2.0) / PATCH * band)[:, None]
        second.append(
            np.concatenate([two(cos[:HALF] * weight), two(sin[:HALF] * weight)], 0)
        )
    first = np.concatenate(first, 0)
    second = np.stack(second)
    return tuple(t.astype(ml_dtypes.bfloat16) for t in (rows, cols, first, second))


def dot(a, b):
    return jnp.dot(a, b, preferred_element_type=jnp.float32)


def centre(position):
    return 8 * position if 8 * position < HALF else 8 * position - PATCH


def kernel(
    n, tile_hbm, place_hbm, mask_ref, use_ref, rows_hbm, cols_hbm, first_hbm, second_hbm,
    out_ref,
    tile_ref, place_ref, rows_ref, cols_ref, first_ref, second_ref, load_sem,
    wide, got, got_mask, own, totals, moments, mine, earlier,
    tile_send, tile_recv, mask_send, mask_recv, flow_send, flow_recv, go, here,
):
    me = lax.axis_index("sec")
    grp = lax.axis_index("grp")
    patches = use_ref.shape[1]
    pairs = patches // 2
    group = GROUP if pairs % GROUP == 0 else 2
    side = tile_ref.shape[1]

    loads = [
        pltpu.make_async_copy(src, dst, load_sem.at[i])
        for i, (src, dst) in enumerate((
            (tile_hbm, tile_ref), (place_hbm, place_ref), (rows_hbm, rows_ref),
            (cols_hbm, cols_ref), (first_hbm, first_ref), (second_hbm, second_ref),
        ))
    ]
    for load in loads:
        load.start()

    barrier = pltpu.get_barrier_semaphore()

    def around(distance, semaphore):
        for other, there in ((me - distance, me >= distance), (me + distance, me + distance < n)):
            @pl.when(there)
            def _(other=other):
                pl.semaphore_signal(semaphore, inc=1, device_id=(grp, other), device_id_type=MESH)

    def await_around(distance, semaphore):
        peers = (me >= distance).astype(jnp.int32) + (me + distance < n).astype(jnp.int32)
        pl.semaphore_wait(semaphore, peers)

    distances = []
    while 2 ** (len(distances) + 1) < n:
        distances.append(2 ** (len(distances) + 1))

    def say(turn):
        if turn < len(distances):
            around(distances[turn], here.at[turn])

    def hear(turn):
        if turn < len(distances):
            await_around(distances[turn], here.at[turn])

    around(1, barrier)
    around(2, barrier)
    loads[0].wait()
    pl.semaphore_wait(barrier, jnp.minimum(me, 2) + jnp.minimum(n - 1 - me, 2))

    def tile_copy(gap):
        return pltpu.make_async_remote_copy(
            src_ref=tile_ref.at[0], dst_ref=got.at[gap - 1],
            send_sem=tile_send.at[gap - 1], recv_sem=tile_recv.at[gap - 1],
            device_id=(grp, me - gap), device_id_type=MESH,
        )

    def mask_copy(gap):
        return pltpu.make_async_remote_copy(
            src_ref=mask_ref, dst_ref=got_mask.at[gap - 1],
            send_sem=mask_send.at[gap - 1], recv_sem=mask_recv.at[gap - 1],
            device_id=(grp, me - gap), device_id_type=MESH,
        )

    odd = lax.rem(me, 2) == 1
    relays = jnp.logical_and(odd, me + 1 < n)
    skips = jnp.logical_and(odd, me >= 2)

    def relay_copy():
        return pltpu.make_async_remote_copy(
            src_ref=got.at[0], dst_ref=got.at[1],
            send_sem=tile_send.at[2], recv_sem=tile_recv.at[1],
            device_id=(grp, me - 1), device_id_type=MESH,
        )

    for gap in (1, 2):
        @pl.when(me >= gap)
        def _(gap=gap):
            if gap == 1:
                tile_copy(gap).start()
            mask_copy(gap).start()
    say(0)

    lane = lax.broadcasted_iota(jnp.int32, (PATCH, PATCH), 1)

    def patch(p):
        row, col = place_ref[0, p], place_ref[1, p]
        block = lax.div(col, PATCH)
        within = lax.rem(col, PATCH)
        a = wide[block, pl.ds(row, PATCH), :]
        b = wide[jnp.minimum(block + 1, side // PATCH - 1), pl.ds(row, PATCH), :]
        mixed = jnp.where(lane >= within, a, b)
        shift = lax.rem(PATCH - within, PATCH)
        return pltpu.roll(mixed, shift, 1).astype(jnp.bfloat16)

    def spectra(q):
        halves = []
        for pair in range(group):
            both = jnp.concatenate([patch(q + pair), patch(q + pair + pairs)], axis=1)
            halves.append(dot(rows_ref[...], both).astype(jnp.bfloat16))
        u = dot(jnp.concatenate([h[:HALF] for h in halves], 0), cols_ref[0])
        v = dot(jnp.concatenate([h[HALF:] for h in halves], 0), cols_ref[1])
        plus, minus = (u + v).astype(jnp.bfloat16), (u - v).astype(jnp.bfloat16)
        return [
            jnp.concatenate([plus[HALF * i:HALF * (i + 1)], minus[HALF * i:HALF * (i + 1)]], 0)
            for i in range(group)
        ]

    def own_quad(i, _):
        for j, value in enumerate(spectra(group * i)):
            own[group * i + j] = value
        return 0

    sub = lax.broadcasted_iota(jnp.int32, (8, 2 * PATCH), 0).astype(jnp.float32)

    def pair_quad(i, _):
        q = group * i
        real, imag = [], []
        for j, other in enumerate(spectra(q)):
            mine_ = own[q + j].astype(jnp.float32)
            other = other.astype(jnp.float32)
            ar, ai = mine_[:, :PATCH], mine_[:, PATCH:]
            br, bi = other[:, :PATCH], other[:, PATCH:]
            real.append((ar * br + ai * bi).astype(jnp.bfloat16))
            imag.append((ai * br - ar * bi).astype(jnp.bfloat16))
        halves = []
        for j in range(0, group, 2):
            cross = jnp.concatenate(
                [jnp.concatenate(real[j:j + 2], 1), jnp.concatenate(imag[j:j + 2], 1)], 0
            )
            halves.append(dot(first_ref[...], cross).astype(jnp.bfloat16))
        for level in range(LEVELS):
            top = 2 * PATCH * level
            both = jnp.concatenate([
                jnp.concatenate([half[top:top + PATCH, lanes], half[top + PATCH:top + 2 * PATCH, lanes]], 1)
                for half in halves for lanes in (slice(0, PATCH), slice(PATCH, 2 * PATCH))
            ], 0)
            correl = dot(both, second_ref[level])
            for j in range(group):
                weights = correl[PATCH * j:PATCH * (j + 1)]
                weights = weights * weights
                total = jnp.zeros((8, 2 * PATCH), jnp.float32)
                moment = jnp.zeros((8, 2 * PATCH), jnp.float32)
                for g in range(PATCH // 8):
                    w = weights[8 * g:8 * (g + 1)]
                    total = total + w
                    if centre(g):
                        moment = moment + w * float(centre(g))
                moment = moment + sub * total
                total = jnp.sum(total, 0, keepdims=True)
                moment = jnp.sum(moment, 0, keepdims=True)
                for h in (0, 1):
                    lanes = slice(PATCH * h, PATCH * (h + 1))
                    totals[level, pl.ds(q + j + h * pairs, 1), :] = total[:, lanes]
                    moments[level, pl.ds(q + j + h * pairs, 1), :] = moment[:, lanes]
        return 0

    position = lax.broadcasted_iota(jnp.int32, (8, PATCH), 1)
    offset = jnp.where(position < HALF, position, position - PATCH).astype(jnp.float32)
    which = lax.broadcasted_iota(jnp.int32, (8, PATCH), 0)
    gather = jnp.where(which == 0, 1.0, jnp.where(which == 1, offset, 0.0))

    def over_lanes(values):
        return lax.dot_general(
            gather, values, (((1,), (1,)), ((), ())),
            precision=lax.Precision.HIGHEST, preferred_element_type=jnp.float32,
        )

    def flow(gap):
        usage = use_ref[...].astype(jnp.float32)
        along_rows = jnp.zeros((1, patches), jnp.float32)
        along_cols = jnp.zeros((1, patches), jnp.float32)
        for level in range(LEVELS):
            whole = over_lanes(totals[level])
            slope = over_lanes(moments[level])
            use = usage[level:level + 1]
            norm = whole[0:1] + 1e-06
            along_rows = along_rows + use * (slope[0:1] / norm)
            along_cols = along_cols + use * (whole[1:2] / norm)
        count = jnp.maximum(jnp.sum(usage, axis=0, keepdims=True), 1.0)
        valid = mask_ref[...].astype(jnp.float32) * got_mask[gap - 1].astype(jnp.float32)
        both = jnp.concatenate([along_rows, along_cols], 0)
        return valid * both / count

    def widen(plane):
        for block in range(side // PATCH):
            lanes = pl.ds(PATCH * block, PATCH)
            wide[block] = plane[:, lanes].astype(jnp.float32)

    widen(tile_ref.at[0])
    for load in loads[1:]:
        load.wait()
    lax.fori_loop(0, pairs // group, own_quad, 0, unroll=2)

    last_pair = jnp.logical_and(me == n - 2, jnp.logical_and(jnp.logical_not(odd), me >= 1))

    @pl.when(last_pair)
    def _():
        tile_copy(1).wait_send()
        pl.semaphore_signal(go, inc=1, device_id=(grp, me + 1), device_id_type=MESH)

    hear(0)
    say(1)

    @pl.when(me + 1 < n)
    def _():
        tile_copy(1).wait_recv()
        pl.when(relays)(lambda: relay_copy().start())
        pl.when(skips)(lambda: tile_copy(2).start())

    hear(1)
    say(2)

    def flow_copy(other):
        return pltpu.make_async_remote_copy(
            src_ref=mine, dst_ref=earlier.at[me],
            send_sem=flow_send.at[other], recv_sem=flow_recv.at[me],
            device_id=(grp, other), device_id_type=MESH,
        )

    for gap, out in ((1, out_ref.at[0]), (2, out_ref.at[1])):
        @pl.when(me + gap < n)
        def _(gap=gap, out=out):
            if gap == 2:
                tile_copy(gap).wait_recv()
            mask_copy(gap).wait_recv()
            widen(got.at[gap - 1])
            lax.fori_loop(0, pairs // group, pair_quad, 0, unroll=2)
            out[0] = flow(gap)

        @pl.when(me + gap >= n)
        def _(gap=gap, out=out):
            if gap == 1:
                @pl.when(skips)
                def _():
                    pl.semaphore_wait(go, 1)
                    tile_copy(2).start()
            out[...] = jnp.zeros_like(out)

        if gap == 1:
            mine[...] = out[0]
            for turn in range(2, len(distances)):
                hear(turn)
                say(turn + 1)

            def send(other, _):
                flow_copy(other).start()
                return 0

            lax.fori_loop(me + 1, n, send, 0)

    def arrived(t, state):
        pltpu.make_async_remote_copy(
            src_ref=mine, dst_ref=earlier.at[t],
            send_sem=flow_send.at[t], recv_sem=flow_recv.at[t],
            device_id=(grp, me), device_id_type=MESH,
        ).wait_recv()
        return state + earlier[t]

    before = lax.fori_loop(0, me, arrived, jnp.zeros(mine.shape, jnp.float32))
    out_ref[2, 0] = before + mine[...]

    def sent(other, _):
        flow_copy(other).wait_send()
        return 0

    lax.fori_loop(me + 1, n, sent, 0)
    for gap in (1, 2):
        @pl.when(me >= gap)
        def _(gap=gap):
            if gap == 1:
                pl.when(jnp.logical_not(last_pair))(lambda: tile_copy(1).wait_send())
            mask_copy(gap).wait_send()
    pl.when(relays)(lambda: relay_copy().wait_send())
    pl.when(skips)(lambda: tile_copy(2).wait_send())


def on_device(n, section_tile, placement, tissue_mask, level_use):
    side = section_tile.shape[1]
    patches = placement.shape[0]
    out = jax.ShapeDtypeStruct((3, 1, 2, patches), jnp.float32)
    vmem = pl.BlockSpec(memory_space=pltpu.VMEM)
    dma = pltpu.SemaphoreType.DMA
    consts = [jnp.asarray(t) for t in tables()]
    anywhere = pl.BlockSpec(memory_space=pl.ANY)
    flows = pl.pallas_call(
        functools.partial(kernel, n),
        out_shape=out,
        in_specs=[anywhere] * 2 + [vmem] * 2 + [anywhere] * 4,
        out_specs=vmem,
        scratch_shapes=[
            pltpu.VMEM(section_tile.shape, section_tile.dtype),
            pltpu.SMEM((2, patches), placement.dtype),
            *[pltpu.VMEM(t.shape, t.dtype) for t in consts],
            dma((6,)),
            pltpu.VMEM((side // PATCH, side, PATCH), jnp.float32),
            pltpu.VMEM((2, side, side), jnp.bfloat16),
            pltpu.VMEM((2, 1, patches), jnp.int32),
            pltpu.VMEM((patches // 2, PATCH, 2 * PATCH), jnp.bfloat16),
            pltpu.VMEM((LEVELS, patches, PATCH), jnp.float32),
            pltpu.VMEM((LEVELS, patches, PATCH), jnp.float32),
            pltpu.VMEM((2, patches), jnp.float32),
            pltpu.VMEM((n, 2, patches), jnp.float32),
            dma((3,)), dma((2,)), dma((2,)), dma((2,)), dma((n,)), dma((n,)), pltpu.SemaphoreType.REGULAR,
            pltpu.SemaphoreType.REGULAR((max(1, n.bit_length()),)),
        ],
        compiler_params=pltpu.CompilerParams(
            collective_id=0, has_side_effects=True, vmem_limit_bytes=56 * 2**20
        ),
    )(section_tile, placement.T, tissue_mask, level_use, *consts)
    return flows[0], flows[1], flows[2]


def solution(mesh):
    in_specs = (
        P(("grp", "sec"), None, None),
        P("grp", None),
        P(("grp", "sec"), None),
        P(None, "grp"),
    )
    out_specs = (P(("grp", "sec"), None, None),) * 3
    return jax.shard_map(
        functools.partial(on_device, mesh.shape["sec"]),
        mesh=mesh, in_specs=in_specs, out_specs=out_specs, check_vma=False,
    )
```
